32 devices in a mesh: groups: 2 (over y), op: 4 (over z), sec: 2 (over x), help: 2 (over core).
Axes of the slice: x: 2, y: 2, z: 4, core: 2. Of those that a mesh axis runs over, the one named last changes fastest.
Arguments:
- psi_one: bfloat16 [16, 256, 256], P(('groups', 'sec'), ('op', 'help')), parts along dimension 0, may hold values from -6 to 6
- psi_two: bfloat16 [16, 256, 256], P(('groups', 'sec'), ('op', 'help')), parts along dimension 0, may hold values from -6 to 6
- left_blocks: bfloat16 [64, 256, 256], P(('groups', 'op')), parts along dimension 0, may hold values from -0.375 to 0.375
- right_blocks: bfloat16 [64, 256, 256], P(('groups', 'op')), parts along dimension 0, may hold values from -0.046875 to 0.046875
- task_in: int32 [8, 2, 64], P(('groups', 'op'), 'sec'), parts along dimension 0, may hold values from 0 to 3
- task_out: int32 [8, 2, 64], P(('groups', 'op'), 'sec'), parts along dimension 0, may hold values from 0 to 3
- task_left: int32 [8, 2, 64], P(('groups', 'op'), 'sec'), parts along dimension 0, may hold values from 0 to 7
- task_right: int32 [8, 2, 64], P(('groups', 'op'), 'sec'), parts along dimension 0, may hold values from 0 to 7
- task_count: int32 [8, 2], P(('groups', 'op'), 'sec'), parts along dimension 0, may hold values from 16 to 64
Outputs:
- sigma_one: float32 [16, 256, 256], P(('groups', 'sec'), ('op', 'help')), parts along dimension 0
- sigma_two: float32 [16, 256, 256], P(('groups', 'sec'), ('op', 'help')), parts along dimension 0
- subspace: float32 [4, 2], P('groups'), parts along dimension 0
The draws below stay inside these ranges and needn't reach their ends.
There are 2 independent parts, one for each index of `groups`. The reference program is written for one: setup_inputs(seed, part) draws one part's arguments, and reference() takes and returns one part's arrays. A program takes and returns all parts, laid end to end along the dimension named above; each array names one. Nothing has to cross between parts.
All inputs are finite; a program needn't handle non-finite values.
Results may differ from the reference program's by a relative error of at most 0.0029.
Values may be sent and summed in bfloat16 or wider, within the bound.
No kernel may reach another device: no remote copies, remote signals or barrier semaphores. Data moves between devices by JAX's collectives and lax.ppermute only.
A program may use at most 64 MiB of HBM per device.

```python
import math
import jax
import jax.numpy as jnp
from jax import lax

B = 256
SEC_DEV = 4
OP_DEV = 8
SLOTS = 64
NSEC = 8
NOPS = 32
N_OP = 4
N_SEC = 2


def place_ends(entries, stream_key, least, largest):
    place = [jax.random.randint(jax.random.fold_in(stream_key, axis), (), 0, length) for axis, length in enumerate(entries.shape)]
    longest = entries.shape.index(max(entries.shape))
    next_to = place[:longest] + [(place[longest] + 1) % entries.shape[longest]] + place[longest + 1:]
    return entries.at[tuple(place)].set(least).at[tuple(next_to)].set(largest)


def block_scale(own_key, extent, split, smallest, high):
    gain = 1.0
    for position, blocks in split:
        steps = jax.random.uniform(jax.random.fold_in(jax.random.fold_in(own_key, 6), position), (blocks,), jnp.float32, smallest / len(split), high / len(split))
        gain = gain * jnp.repeat(jnp.exp(steps), extent[position] // blocks).reshape((-1,) + (1,) * (len(extent) - 1 - position))
    return gain


def scatter_about(stream_key, shape, scale, reach, shards=(), kind=jnp.bfloat16):
    gain = block_scale(stream_key, shape, shards, -0.22, 0.18) if shards else 1.0
    drawn = jax.random.normal(stream_key, shape, jnp.float32) * scale * gain
    return jnp.minimum(jnp.maximum(drawn, -reach), reach).astype(kind)


def setup_inputs(seed: int = 0, part: int = 0) -> dict:
    seeds = jax.random.split(jax.random.key(seed), 10)
    part_keys = jax.random.split(jax.random.fold_in(seeds[9], part), 10)
    return {
        "psi_one": scatter_about(part_keys[0], (NSEC, B, B), 1.0, 6.0, ((0, 2), (1, 8))),
        "psi_two": scatter_about(part_keys[1], (NSEC, B, B), 1.0, 6.0, ((0, 2), (1, 8))),
        "left_blocks": scatter_about(part_keys[2], (NOPS, B, B), B ** -0.5, 0.375, ((0, 4),)),
        "right_blocks": scatter_about(part_keys[3], (NOPS, B, B), (B * SLOTS * N_OP // SEC_DEV) ** -0.5, 0.046875, ((0, 4),)),
        "task_in": place_ends(jax.random.randint(part_keys[4], (N_OP, N_SEC, SLOTS), 0, SEC_DEV), jax.random.fold_in(part_keys[4], 1), 0, SEC_DEV - 1).astype(jnp.int32),
        "task_out": place_ends(jax.random.randint(part_keys[5], (N_OP, N_SEC, SLOTS), 0, SEC_DEV), jax.random.fold_in(part_keys[5], 1), 0, SEC_DEV - 1).astype(jnp.int32),
        "task_left": place_ends(jax.random.randint(part_keys[6], (N_OP, N_SEC, SLOTS), 0, OP_DEV), jax.random.fold_in(part_keys[6], 1), 0, OP_DEV - 1).astype(jnp.int32),
        "task_right": place_ends(jax.random.randint(part_keys[7], (N_OP, N_SEC, SLOTS), 0, OP_DEV), jax.random.fold_in(part_keys[7], 1), 0, OP_DEV - 1).astype(jnp.int32),
        "task_count": place_ends(jax.random.randint(part_keys[8], (N_OP, N_SEC), SLOTS // 4, SLOTS + 1), jax.random.fold_in(part_keys[8], 1), SLOTS // 4, SLOTS).astype(jnp.int32),
    }


def reference(psi_one, psi_two, left_blocks, right_blocks, task_in, task_out, task_left, task_right, task_count):
    waves = jnp.stack([psi_one, psi_two])
    group_ids = jnp.broadcast_to(jnp.arange(N_OP, dtype=jnp.int32)[:, None, None], task_in.shape)
    owner_ids = jnp.broadcast_to(jnp.arange(N_SEC, dtype=jnp.int32)[None, :, None], task_in.shape)
    slot_ids = jnp.broadcast_to(jnp.arange(SLOTS, dtype=jnp.int32)[None, None, :], task_in.shape)
    live = (slot_ids < task_count[:, :, None]).reshape(-1)
    sector_in = (owner_ids * SEC_DEV + task_in).reshape(-1).astype(jnp.int32)
    sector_out = (owner_ids * SEC_DEV + task_out).reshape(-1).astype(jnp.int32)
    left_ids = (group_ids * OP_DEV + task_left).reshape(-1).astype(jnp.int32)
    right_ids = (group_ids * OP_DEV + task_right).reshape(-1).astype(jnp.int32)

    def add_task(sigma, item):
        src, dst, lidx, ridx, alive = item
        block = lax.dynamic_index_in_dim(waves, src, 1, keepdims=False).astype(jnp.float32)
        left = lax.dynamic_index_in_dim(left_blocks, lidx, 0, keepdims=False).astype(jnp.float32)
        right = lax.dynamic_index_in_dim(right_blocks, ridx, 0, keepdims=False).astype(jnp.float32)
        inner = jnp.einsum('ij,vjk->vik', left, block).astype(jnp.bfloat16)
        contrib = jnp.einsum('vik,lk->vil', inner.astype(jnp.float32), right)
        contrib = jnp.where(alive, contrib, jnp.zeros_like(contrib))
        old = lax.dynamic_index_in_dim(sigma, dst, 1, keepdims=False)
        sigma = lax.dynamic_update_index_in_dim(sigma, old + contrib, dst, 1)
        return (sigma, None)
    start = jnp.zeros((2, NSEC, B, B), jnp.float32)
    sigma, _ = lax.scan(add_task, start, (sector_in, sector_out, left_ids, right_ids, live))
    dots = jnp.einsum('vsab,wsab->vw', waves.astype(jnp.float32), sigma, precision=lax.Precision.HIGHEST)
    subspace = dots / math.sqrt(NSEC * B * B)
    return (sigma[0], sigma[1], subspace)
```

```python
import functools
import math

import jax
import jax.numpy as jnp
from jax import lax
from jax.experimental import pallas as pl
from jax.experimental.pallas import tpu as pltpu
from jax.sharding import PartitionSpec as P

GROUP = 4
F32 = jnp.float32
BF16 = jnp.bfloat16
SMEM = pltpu.SMEM
VMEM = pltpu.VMEM


def plan_kernel(sectors, ops, slots, inputs, targets, lefts, rights, count, block_ref, right_ref, starts_ref):
    live = count[0]
    spare = sectors * ops

    def tally(t, tallies):
        here = jnp.where(t < live, targets[t], sectors)
        return tuple(n + jnp.where(here == c, 1, 0) for c, n in enumerate(tallies))

    tallies = lax.fori_loop(0, slots, tally, tuple(jnp.int32(0) for _ in range(sectors)))
    first = jnp.int32(0)
    begins = []
    for c in range(sectors):
        begins.append(first)
        starts_ref[c] = first // GROUP
        padded = (tallies[c] + GROUP - 1) // GROUP * GROUP
        for i in range(GROUP):
            block_ref[first + tallies[c] + i] = spare
            right_ref[first + tallies[c] + i] = 0
        first = first + padded
    starts_ref[sectors] = first // GROUP

    def place(t, cursors):
        here = targets[t]
        at = jnp.int32(0)
        for c in range(sectors):
            at = jnp.where(here == c, cursors[c], at)
        block_ref[at] = inputs[t] * ops + lefts[t]
        right_ref[at] = rights[t]
        return tuple(n + jnp.where(here == c, 1, 0) for c, n in enumerate(cursors))

    lax.fori_loop(0, live, place, tuple(begins))


def make_plan(sectors, ops, slots, tasks, count):
    room = slots + 2 * sectors * GROUP + GROUP
    spec = pl.BlockSpec(memory_space=SMEM)
    return pl.pallas_call(
        functools.partial(plan_kernel, sectors, ops, slots),
        out_shape=(
            jax.ShapeDtypeStruct((room,), jnp.int32),
            jax.ShapeDtypeStruct((room,), jnp.int32),
            jax.ShapeDtypeStruct((sectors + 1,), jnp.int32),
        ),
        in_specs=[spec] * 5,
        out_specs=(spec,) * 3,
        name="plan",
    )(*tasks, count)


def tile_of(x):
    total = None
    for r in range(0, x.shape[0], 8):
        for c in range(0, x.shape[1], 128):
            part = x[r : r + 8, c : c + 128]
            total = part if total is None else total + part
    return total


def product_kernel(n_op, in_place, place, block, right, starts, left_ref, right_ref, *refs):
    n_in = 2 * n_op if in_place else 1
    waves_in, refs = refs[:n_in], refs[n_in:]
    n_out = n_op if in_place else 1
    outs, (dots_ref, waves, inner, sums) = refs[:n_out], refs[n_out:]
    _, sectors, width, _ = waves.shape
    ops = left_ref.shape[0]
    half = left_ref.shape[1] * left_ref.shape[2]
    rows = left_ref.shape[2]
    me, helper = place[0], place[1]
    if in_place:
        for k in range(n_op):
            origin = lax.rem(me - k + n_op, n_op)
            for other in range(2):
                owner = helper if other == 0 else 1 - helper
                at = pl.multiple_of((origin * 2 + owner) * rows, rows)
                waves[:, :, pl.ds(at, rows), :] = waves_in[other * n_op + k][...]
    else:
        waves[...] = waves_in[0][...]
    left = left_ref[...].reshape(ops * half, width)
    for a in range(sectors):
        for v in range(2):
            found = jnp.dot(left, waves[v, a], preferred_element_type=F32).astype(BF16)
            inner[pl.ds(a * ops, ops), v] = found.reshape(ops, half, width)
    inner[sectors * ops] = jnp.zeros((2, half, width), BF16)
    sums[...] = jnp.zeros_like(sums)
    for c in range(sectors):

        def step(g, carry, c=c):
            total = sums[c]
            for i in range(GROUP):
                total = total + lax.dot_general(
                    inner[block[g * GROUP + i]].reshape(2 * half, width),
                    right_ref[right[g * GROUP + i]],
                    (((1,), (1,)), ((), ())),
                    preferred_element_type=F32,
                ).reshape(2, n_op, rows, width)
            sums[c] = total
            return carry

        lax.fori_loop(starts[c], starts[c + 1], step, 0)
    dots = [[None, None], [None, None]]
    for c in range(sectors):
        for origin in range(n_op):
            at = pl.multiple_of((origin * 2 + helper) * rows, rows)
            for v in range(2):
                wave = waves[v, c, pl.ds(at, rows), :].astype(F32)
                for w in range(2):
                    part = tile_of(wave * sums[c, w, origin])
                    dots[v][w] = part if dots[v][w] is None else dots[v][w] + part
    row = lax.broadcasted_iota(jnp.int32, (8, 128), 0)
    lane = lax.broadcasted_iota(jnp.int32, (8, 128), 1)
    tile = jnp.zeros((8, 128), F32)
    for v in range(2):
        for w in range(2):
            tile = jnp.where((row == v) & (lane == w), jnp.sum(dots[v][w]), tile)
    dots_ref[...] = tile
    if in_place:
        for k in range(n_op):
            goal = lax.rem(me + k, n_op)
            for c in range(sectors):
                for v in range(2):
                    outs[k][v, c] = sums[c, v, goal].astype(outs[k].dtype)
    else:
        outs[0][...] = sums[...]


def products(n_op, in_place, place, plan, left_blocks, right_blocks, waves, sectors, rows):
    ops, width, _ = right_blocks.shape
    half = n_op * rows
    if in_place:
        outs = [jax.ShapeDtypeStruct((2, sectors, rows, width), F32 if k == 0 else BF16) for k in range(n_op)]
    else:
        outs = [jax.ShapeDtypeStruct((sectors, 2, n_op, rows, width), F32)]
    outs.append(jax.ShapeDtypeStruct((8, 128), F32))

    left_spec = pl.BlockSpec((ops, n_op, None, rows, width), lambda i, place, *_: (0, 0, place[1], 0, 0))
    full = lambda s: pl.BlockSpec(s, lambda i, *_: (0,) * len(s))
    grid_spec = pltpu.PrefetchScalarGridSpec(
        num_scalar_prefetch=4,
        grid=(1,),
        in_specs=[left_spec, full(right_blocks.shape)] + [full(w.shape) for w in waves],
        out_specs=[full(o.shape) for o in outs],
        scratch_shapes=[
            pltpu.VMEM((2, sectors, width, width), BF16),
            pltpu.VMEM((sectors * ops + 1, 2, half, width), BF16),
            pltpu.VMEM((sectors, 2, n_op, rows, width), F32),
        ],
    )
    return pl.pallas_call(
        functools.partial(product_kernel, n_op, in_place),
        out_shape=outs,
        grid_spec=grid_spec,
        compiler_params=pltpu.CompilerParams(vmem_limit_bytes=48 * 1024 * 1024),
        name="products",
    )(place, *plan, left_blocks, right_blocks, *waves)


def finish_kernel(scale, n, own_ref, dots_ref, *refs):
    others, (one_ref, two_ref, subspace_ref) = refs[:n], refs[n:]
    for v, out in enumerate((one_ref, two_ref)):
        total = own_ref[v]
        for other in others:
            total = total + other[v].astype(F32)
        out[...] = total
    subspace_ref[...] = dots_ref[:2, :2] * scale


def finish(scale, own, others, dots):
    _, sectors, rows, width = own.shape
    whole = pl.BlockSpec(memory_space=VMEM)
    out = jax.ShapeDtypeStruct((sectors, rows, width), F32)
    return pl.pallas_call(
        functools.partial(finish_kernel, scale, len(others)),
        out_shape=(out, out, jax.ShapeDtypeStruct((2, 2), F32)),
        in_specs=[whole] * (2 + len(others)),
        out_specs=(whole,) * 3,
        name="finish",
    )(own, dots, *others)


def sum_over(x, axis):
    size = lax.axis_size(axis)
    if size & (size - 1):
        return lax.psum(x, axis)
    hop = 1
    while hop < size:
        x = x + lax.ppermute(x, axis, [(i, i ^ hop) for i in range(size)])
        hop *= 2
    return x


def local(
    psi_one,
    psi_two,
    left_blocks,
    right_blocks,
    task_in,
    task_out,
    task_left,
    task_right,
    task_count,
):
    sectors, rows, width = psi_one.shape
    ops = left_blocks.shape[0]
    slots = task_in.shape[-1]
    n_op = lax.axis_size("op")
    me = lax.axis_index("op")
    helper = lax.axis_index("help")
    in_place = rows % 16 == 0
    place = jnp.stack([me, helper]).astype(jnp.int32)
    tasks = [t.reshape(slots) for t in (task_in, task_out, task_left, task_right)]
    plan = make_plan(sectors, ops, slots, tasks, task_count.reshape(1))
    shift = lambda x, k: lax.ppermute(x, "op", [(i, (i + k) % n_op) for i in range(n_op)])
    swap = lambda x: lax.ppermute(x, "help", [(0, 1), (1, 0)])
    own = jnp.stack([psi_one, psi_two])
    if in_place:
        near = [own] + [shift(own, k) for k in range(1, n_op)]
        waves = near + [swap(x) for x in near]
    else:
        waves = [lax.all_gather(own, ("op", "help"), axis=2, tiled=True)]
    lefts = left_blocks.reshape(ops, n_op, 2, rows, width)
    *parts, dots = products(n_op, in_place, place, plan, lefts, right_blocks, waves, sectors, rows)
    if not in_place:
        sums = jnp.moveaxis(parts[0], 2, 0).swapaxes(1, 2)
        picked = [jnp.take(sums, (me + k) % n_op, axis=0) for k in range(n_op)]
        parts = [p if k == 0 else p.astype(BF16) for k, p in enumerate(picked)]
    others = [shift(parts[k], k) for k in range(1, n_op)]
    for axis in ("help", "sec", "op"):
        dots = sum_over(dots, axis)
    scale = 1.0 / math.sqrt(sectors * lax.axis_size("sec") * width * width)
    return finish(scale, parts[0], others, dots)


def solution(mesh):
    placed = (
        P(("groups", "sec"), ("op", "help"), None),
        P(("groups", "sec"), ("op", "help"), None),
        P(("groups", "op"), None, None),
        P(("groups", "op"), None, None),
        P(("groups", "op"), "sec", None),
        P(("groups", "op"), "sec", None),
        P(("groups", "op"), "sec", None),
        P(("groups", "op"), "sec", None),
        P(("groups", "op"), "sec"),
    )
    return jax.shard_map(
        local,
        mesh=mesh,
        in_specs=placed,
        out_specs=(
            P(("groups", "sec"), ("op", "help"), None),
            P(("groups", "sec"), ("op", "help"), None),
            P("groups", None),
        ),
        check_vma=False,
    )
```

```python
import functools
import math

import jax
import jax.numpy as jnp
from jax import lax
from jax.experimental import pallas as pl
from jax.experimental.pallas import tpu as pltpu
from jax.sharding import PartitionSpec as P

F32 = jnp.float32
BF16 = jnp.bfloat16
SCALARS = pl.BlockSpec(memory_space=pltpu.SMEM)
VECTORS = pl.BlockSpec(memory_space=pltpu.VMEM)
MIB = 1024 * 1024


def call(kernel, outs, args, n_scalars, mib, name, scratch=(), flops=0):
    return pl.pallas_call(
        kernel,
        out_shape=outs,
        in_specs=[SCALARS] * n_scalars + [VECTORS] * (len(args) - n_scalars),
        out_specs=jax.tree.map(lambda _: VECTORS, outs),
        scratch_shapes=list(scratch),
        compiler_params=pltpu.CompilerParams(vmem_limit_bytes=mib * MIB),
        cost_estimate=pl.CostEstimate(flops=flops, bytes_accessed=0, transcendentals=0) if flops else None,
        name=name,
    )(*args)


def tile_of(x):
    total = None
    for r in range(0, x.shape[0], 8):
        for c in range(0, x.shape[1], 128):
            part = x[r : r + 8, c : c + 128]
            total = part if total is None else total + part
    return total


def dots_of(me, near, sums):
    sectors, n_op = sums[0].shape[:2]
    dots = [[None, None], [None, None]]
    for k in range(n_op):
        for c in range(sectors):
            parts = [s[c, me ^ k] for s in sums]
            for v in range(2):
                wave = near[v][k][c].astype(F32)
                for w in range(2):
                    part = tile_of(wave * parts[w])
                    dots[v][w] = part if dots[v][w] is None else dots[v][w] + part
    return spread(dots)


def spread(dots):
    row = lax.broadcasted_iota(jnp.int32, (8, 128), 0)
    lane = lax.broadcasted_iota(jnp.int32, (8, 128), 1)
    tile = jnp.zeros((8, 128), F32)
    for v in range(2):
        for w in range(2):
            tile = jnp.where((row == v) & (lane == w), jnp.sum(dots[v][w]), tile)
    return tile


def to_wire(tile, width):
    high = tile.astype(BF16).astype(F32)
    middle = (tile - high).astype(BF16).astype(F32)
    low = tile - high - middle
    parts = jnp.concatenate([high[:2], middle[:2], low[:2], jnp.zeros((10, 128), F32)])
    return jnp.concatenate([parts] * (width // 128), axis=1).astype(BF16)


def from_wire(ref, at):
    parts = ref[at:, :128].astype(F32)
    two = parts[0:2] + parts[2:4] + parts[4:6]
    return jnp.concatenate([two, jnp.zeros((6, 128), F32)])


def add_tasks(batch, table, left_ref, right_ref, waves, inner, sums):
    sectors, n_op, rows, width = sums.shape
    ops, half = right_ref.shape[0], n_op * rows
    left = left_ref[...].reshape(ops * half, width)
    for a in range(sectors):
        found = jnp.dot(left, waves[a], preferred_element_type=F32).astype(BF16)
        inner[pl.ds(a * ops, ops)] = found.reshape(ops, half, width)
    inner[sectors * ops] = jnp.zeros((half, width), BF16)
    sums[...] = jnp.zeros_like(sums)

    def step(g, carry):
        for i in range(batch):
            t = g * batch + i
            found = jnp.dot(inner[table[0, t]], right_ref[table[1, t]], preferred_element_type=F32)
            sums[table[2, t]] += found.reshape(n_op, rows, width)
        return carry

    lax.fori_loop(0, (table[3, 2] + batch - 1) // batch, step, 0)


def fast_kernel(batch, last, table, left_ref, right_ref, *refs):
    waves_in, refs = refs[:8], refs[8:]
    if last:
        near_one, sums_one, refs = refs[:4], refs[4], refs[5:]
        sums, sent, dots_ref, waves, inner = refs
    else:
        sums, sent, waves, inner = refs
    rows = sums.shape[2]
    me, helper = table[3, 0], table[3, 1]
    for k in range(4):
        for other in range(2):
            owner = helper if other == 0 else 1 - helper
            at = pl.multiple_of(((me ^ k) * 2 + owner) * rows, rows)
            waves[:, pl.ds(at, rows), :] = waves_in[other * 4 + k][...]
    add_tasks(batch, table, left_ref, right_ref, waves, inner, sums)
    n = sums.shape[0] * rows
    for i, k in enumerate((1, 3)):
        sent[i * n : (i + 1) * n] = sums[:, me ^ k].reshape(n, -1).astype(BF16)
    if last:
        tile = dots_of(me, (near_one, waves_in[:4]), (sums_one, sums))
        dots_ref[...] = tile
        sent[2 * n :] = to_wire(tile, sent.shape[1])


def fast_products(batch, table, left, right, waves, earlier=()):
    ops, n_op, rows, width = left.shape
    sectors = waves[0].shape[0]
    outs = [jax.ShapeDtypeStruct((sectors, n_op, rows, width), F32)]
    extra = 16 if earlier else 0
    outs.append(jax.ShapeDtypeStruct((2 * sectors * rows + extra, width), BF16))
    if earlier:
        outs.append(jax.ShapeDtypeStruct((8, 128), F32))
    scratch = [
        pltpu.VMEM((sectors, width, width), BF16),
        pltpu.VMEM((sectors * ops + 1, n_op * rows, width), BF16),
    ]
    kernel = functools.partial(fast_kernel, batch, bool(earlier))
    return call(kernel, outs, [table, left, right, *waves, *earlier], 1, 12, "products", scratch)


def any_kernel(batch, table, left_ref, right_ref, waves, sums, inner):
    add_tasks(batch, table, left_ref, right_ref, waves, inner, sums)


def any_products(batch, table, left, right, waves):
    ops, n_op, rows, width = left.shape
    sectors = waves.shape[0]
    out = jax.ShapeDtypeStruct((sectors, n_op, rows, width), F32)
    scratch = [pltpu.VMEM((sectors * ops + 1, n_op * rows, width), BF16)]
    kernel = functools.partial(any_kernel, batch)
    return call(kernel, out, [table, left, right, waves], 1, 12, "products", scratch)


def add_up(terms):
    while len(terms) > 1:
        terms = [a + b for a, b in zip(terms[::2], terms[1::2])]
    return terms[0]


def pair_kernel(last, table, sums, received, *refs):
    part = sums[:, table[3, 0] ^ 2]
    n = part.shape[0] * part.shape[1]
    total = part.reshape(n, -1) + received[n : 2 * n].astype(F32)
    if last:
        dots, out, dots_out = refs
        tile = dots[...] + from_wire(received, 2 * n)
        dots_out[...] = tile
        out[n:] = to_wire(tile, out.shape[1])
    else:
        (out,) = refs
    out[:n] = total.astype(BF16)


def pair_sums(table, sums, received, dots=()):
    sectors, _, rows, width = sums.shape
    outs = [jax.ShapeDtypeStruct((sectors * rows + 16 * len(dots), width), BF16)]
    outs += [jax.ShapeDtypeStruct((8, 128), F32)] * len(dots)
    args = [table, sums, received, *dots]
    return call(functools.partial(pair_kernel, bool(dots)), outs, args, 1, 2, "pair_sums")


def dots_kernel(n, dots, far, out):
    out[...] = dots[...] + from_wire(far, n)


def all_dots(dots, far):
    kernel = functools.partial(dots_kernel, far.shape[0] - 16)
    return call(kernel, jax.ShapeDtypeStruct((8, 128), F32), [dots, far], 0, 1, "all_dots")


def finish_kernel(table, sums, received, far, out):
    n = out.shape[0] * out.shape[1]
    near = (received[:n].astype(F32) + far[:n].astype(F32)).reshape(out.shape)
    out[...] = sums[:, table[3, 0]] + near


def finish(table, sums, received, far):
    sectors, _, rows, width = sums.shape
    out = jax.ShapeDtypeStruct((sectors, rows, width), F32)
    return call(finish_kernel, out, [table, sums, received, far], 1, 3, "finish")


def subspace_kernel(scale, *refs):
    refs[-1][...] = add_up([t[:2, :2] for t in refs[:-1]]) * scale


def subspace_of(scale, terms):
    out = jax.ShapeDtypeStruct((2, 2), F32)
    return call(functools.partial(subspace_kernel, scale), out, terms, 0, 1, "subspace")


def terms_of(x, axes):
    size = math.prod(lax.axis_size(a) for a in axes)
    terms, hop = [x], 1
    while hop < size:
        x = add_up(terms)
        hops = [hop] if hop * 2 == size else [hop, 2 * hop, 3 * hop]
        terms = [x] + [swap(x, axes, h) for h in hops]
        hop *= 1 + len(hops)
    return terms


def swap(x, axes, hop):
    size = math.prod(lax.axis_size(a) for a in axes)
    return lax.ppermute(x, axes, [(i, i ^ hop) for i in range(size)])


def after(x, y):
    return lax.optimization_barrier((x, y))


def fast(psi_one, psi_two, left, right, table, batch, scale):
    op, core = ("op",), ("help",)
    far_one = swap(psi_one, op, 2)
    (one, two), left = after((psi_one, psi_two), left)
    far_two = swap(two, op, 2)
    two, far_one = after(two, far_one)
    near = [
        [psi_one, swap(one, op, 1), far_one, swap(far_one, op, 1)],
        [psi_two, swap(two, op, 1), far_two, swap(far_two, op, 1)],
    ]
    sums, received = [], []
    for v in range(2):
        ready = near[v]
        if v == 1:
            ready, sums = after(near[v], sums)
        waves = ready + [swap(x, core, 1) for x in ready]
        earlier = [*near[0], sums[0]] if v == 1 else ()
        total, sent, *dots = fast_products(batch, table, left, right, waves, earlier)
        sums.append(total)
        received.append(swap(sent, op, 1))
    (sent,) = pair_sums(table, sums[0], received[0])
    far_one = swap(sent, op, 2)
    sent, tile = pair_sums(table, sums[1], received[1], dots)
    far_two = swap(sent, op, 2)
    terms = terms_of(all_dots(tile, far_two), ("sec", "help"))
    sigma_one = finish(table, sums[0], received[0], far_one)
    sigma_two = finish(table, sums[1], received[1], far_two)
    return sigma_one, sigma_two, subspace_of(scale, terms)


def general(psi_one, psi_two, left, right, table, batch, scale):
    n_op = lax.axis_size("op")
    me = lax.axis_index("op")
    own = jnp.stack([psi_one, psi_two])
    waves = lax.all_gather(own, ("op", "help"), axis=2, tiled=True)
    sums = jnp.stack([any_products(batch, table, left, right, waves[v]) for v in range(2)])
    total = jnp.take(sums, me, axis=2)
    for k in range(1, n_op):
        sent = jnp.take(sums, (me + k) % n_op, axis=2).astype(BF16)
        moved = lax.ppermute(sent, "op", [(i, (i + k) % n_op) for i in range(n_op)])
        total = total + moved.astype(F32)
    rows = psi_one.shape[1]
    parts = waves.reshape(*waves.shape[:2], n_op, 2, rows, waves.shape[-1])
    mine = jnp.take(parts, lax.axis_index("help"), axis=3).astype(F32)
    dots = jnp.einsum("vsoab,wsoab->vw", mine, sums, precision=lax.Precision.HIGHEST)
    return total[0], total[1], lax.psum(dots, ("op", "sec", "help")) * scale


def local(
    psi_one,
    psi_two,
    left_blocks,
    right_blocks,
    task_in,
    task_out,
    task_left,
    task_right,
    task_count,
):
    sectors, rows, width = psi_one.shape
    ops = left_blocks.shape[0]
    slots = task_in.shape[-1]
    n_op = lax.axis_size("op")
    me = lax.axis_index("op")
    helper = lax.axis_index("help")
    slot = jnp.arange(slots, dtype=jnp.int32)
    flat = lambda t: t.reshape(slots)
    live = task_count.reshape(())
    block = jnp.where(slot < live, flat(task_in) * ops + flat(task_left), sectors * ops)
    state = jnp.where(slot == 0, me, jnp.where(slot == 1, helper, live)).astype(jnp.int32)
    table = jnp.stack([block, flat(task_right), flat(task_out), state])
    lefts = left_blocks.reshape(ops, n_op, 2, rows, width)
    left = jnp.take(lefts, helper, axis=2)
    right = jnp.swapaxes(right_blocks, 1, 2)
    batch = math.gcd(slots, 16)
    scale = 1.0 / math.sqrt(sectors * lax.axis_size("sec") * width * width)
    way = fast if n_op == 4 and rows % 16 == 0 else general
    return way(psi_one, psi_two, left, right, table, batch, scale)


def solution(mesh):
    placed = (
        P(("groups", "sec"), ("op", "help"), None),
        P(("groups", "sec"), ("op", "help"), None),
        P(("groups", "op"), None, None),
        P(("groups", "op"), None, None),
        P(("groups", "op"), "sec", None),
        P(("groups", "op"), "sec", None),
        P(("groups", "op"), "sec", None),
        P(("groups", "op"), "sec", None),
        P(("groups", "op"), "sec"),
    )
    return jax.shard_map(
        local,
        mesh=mesh,
        in_specs=placed,
        out_specs=(
            P(("groups", "sec"), ("op", "help"), None),
            P(("groups", "sec"), ("op", "help"), None),
            P("groups", None),
        ),
        check_vma=False,
    )
```

```python
import functools
import math

import jax
import jax.numpy as jnp
from jax import lax
from jax.experimental import pallas as pl
from jax.experimental.pallas import tpu as pltpu
from jax.sharding import PartitionSpec as P

F32 = jnp.float32
BF16 = jnp.bfloat16
SCALARS = pl.BlockSpec(memory_space=pltpu.SMEM)
VECTORS = pl.BlockSpec(memory_space=pltpu.VMEM)
MIB = 1024 * 1024


def call(kernel, outs, args, n_scalars, mib, name, scratch=(), flops=0):
    return pl.pallas_call(
        kernel,
        out_shape=outs,
        in_specs=[SCALARS] * n_scalars + [VECTORS] * (len(args) - n_scalars),
        out_specs=jax.tree.map(lambda _: VECTORS, outs),
        scratch_shapes=list(scratch),
        compiler_params=pltpu.CompilerParams(vmem_limit_bytes=mib * MIB),
        cost_estimate=pl.CostEstimate(flops=flops, bytes_accessed=0, transcendentals=0) if flops else None,
        name=name,
    )(*args)


def tile_of(x):
    total = None
    for r in range(0, x.shape[0], 8):
        for c in range(0, x.shape[1], 128):
            part = x[r : r + 8, c : c + 128]
            total = part if total is None else total + part
    return total


def dots_of(me, near, sums):
    sectors, n_op = sums.shape[0], sums.shape[2]
    dots = [[None, None], [None, None]]
    for k in range(n_op):
        for c in range(sectors):
            parts = [sums[c, w, me ^ k] for w in range(2)]
            for v in range(2):
                wave = near[v][k][c].astype(F32)
                for w in range(2):
                    part = tile_of(wave * parts[w])
                    dots[v][w] = part if dots[v][w] is None else dots[v][w] + part
    row = lax.broadcasted_iota(jnp.int32, (8, 128), 0)
    lane = lax.broadcasted_iota(jnp.int32, (8, 128), 1)
    tile = jnp.zeros((8, 128), F32)
    for v in range(2):
        for w in range(2):
            tile = jnp.where((row == v) & (lane == w), jnp.sum(dots[v][w]), tile)
    return tile


def to_wire(tile, width):
    high = tile.astype(BF16).astype(F32)
    middle = (tile - high).astype(BF16).astype(F32)
    low = tile - high - middle
    parts = jnp.concatenate([high[:2], middle[:2], low[:2], jnp.zeros((10, 128), F32)])
    return jnp.concatenate([parts] * (width // 128), axis=1).astype(BF16)


def from_wire(ref, at):
    parts = ref[at:, :128].astype(F32)
    two = parts[0:2] + parts[2:4] + parts[4:6]
    return jnp.concatenate([two, jnp.zeros((6, 128), F32)])


def add_tasks(batch, table, left_ref, right_ref, waves, inner, sums):
    sectors, _, n_op, rows, width = sums.shape
    ops, half = right_ref.shape[0], n_op * rows
    left = left_ref[...].reshape(ops * half, width)
    for a in range(sectors):
        for v in range(2):
            found = jnp.dot(left, waves[v, a], preferred_element_type=F32).astype(BF16)
            inner[pl.ds(a * ops, ops), v] = found.reshape(ops, half, width)
    inner[sectors * ops] = jnp.zeros((2, half, width), BF16)
    sums[...] = jnp.zeros_like(sums)

    def step(g, carry):
        for i in range(batch):
            t = g * batch + i
            block = inner[table[0, t]].reshape(2 * half, width)
            found = jnp.dot(block, right_ref[table[1, t]], preferred_element_type=F32)
            sums[table[2, t]] += found.reshape(2, n_op, rows, width)
        return carry

    lax.fori_loop(0, (table[3, 2] + batch - 1) // batch, step, 0)


def fast_kernel(batch, table, left_ref, right_ref, *refs):
    waves_in, refs = refs[:16], refs[16:]
    *outs, dots_ref, waves, inner, sums = refs
    rows = sums.shape[3]
    me, helper = table[3, 0], table[3, 1]
    for v in range(2):
        for k in range(4):
            for other in range(2):
                owner = helper if other == 0 else 1 - helper
                at = pl.multiple_of(((me ^ k) * 2 + owner) * rows, rows)
                waves[v, :, pl.ds(at, rows), :] = waves_in[v * 8 + other * 4 + k][...]
    add_tasks(batch, table, left_ref, right_ref, waves, inner, sums)
    n = sums.shape[0] * rows
    for v in range(2):
        for k in range(4):
            part = sums[:, v, me ^ k].reshape(n, -1)
            outs[4 * v + k][:n] = part if k == 0 else part.astype(BF16)
    tile = dots_of(me, (waves_in[:4], waves_in[8:12]), sums)
    dots_ref[...] = tile
    wire = to_wire(tile, sums.shape[-1])
    for k in range(1, 4):
        outs[k][n:] = wire


def fast_products(batch, table, left, right, waves):
    ops, n_op, rows, width = left.shape
    sectors = waves[0].shape[0]
    outs = []
    for v in range(2):
        n = sectors * rows
        outs.append(jax.ShapeDtypeStruct((n, width), F32))
        outs += [jax.ShapeDtypeStruct((n + (16 if v == 0 else 0), width), BF16)] * 3
    outs.append(jax.ShapeDtypeStruct((8, 128), F32))
    scratch = [
        pltpu.VMEM((2, sectors, width, width), BF16),
        pltpu.VMEM((sectors * ops + 1, 2, n_op * rows, width), BF16),
        pltpu.VMEM((sectors, 2, n_op, rows, width), F32),
    ]
    kernel = functools.partial(fast_kernel, batch)
    return call(kernel, outs, [table, left, right, *waves], 1, 20, "products", scratch)


def any_kernel(batch, table, left_ref, right_ref, waves, sums, inner):
    add_tasks(batch, table, left_ref, right_ref, waves, inner, sums)


def any_products(batch, table, left, right, waves):
    ops, n_op, rows, width = left.shape
    sectors = waves.shape[1]
    out = jax.ShapeDtypeStruct((sectors, 2, n_op, rows, width), F32)
    scratch = [pltpu.VMEM((sectors * ops + 1, 2, n_op * rows, width), BF16)]
    kernel = functools.partial(any_kernel, batch)
    return call(kernel, out, [table, left, right, waves], 1, 20, "products", scratch)


def add_up(terms):
    while len(terms) > 1:
        terms = [a + b for a, b in zip(terms[::2], terms[1::2])]
    return terms[0]


def dots_kernel(n, own, *refs):
    refs[-1][...] = add_up([own[...]] + [from_wire(r, n) for r in refs[:-1]])


def all_dots(own, received):
    kernel = functools.partial(dots_kernel, received[0].shape[0] - 16)
    return call(kernel, jax.ShapeDtypeStruct((8, 128), F32), [own, *received], 0, 1, "all_dots")


def finish_kernel(mine, *refs):
    received, out = refs[:-1], refs[-1]
    n = mine.shape[0]
    total = mine[...]
    for part in received:
        total = total + part[:n].astype(F32)
    out[...] = total.reshape(out.shape)


def finish(shape, mine, received):
    out = jax.ShapeDtypeStruct(shape, F32)
    return call(finish_kernel, out, [mine, *received], 0, 4, "finish")


def subspace_kernel(scale, *refs):
    refs[-1][...] = add_up([t[:2, :2] for t in refs[:-1]]) * scale


def subspace_of(scale, terms):
    out = jax.ShapeDtypeStruct((2, 2), F32)
    return call(functools.partial(subspace_kernel, scale), out, terms, 0, 1, "subspace")


def terms_of(x, axes):
    size = math.prod(lax.axis_size(a) for a in axes)
    terms, hop = [x], 1
    while hop < size:
        x = add_up(terms)
        hops = [hop] if hop * 2 == size else [hop, 2 * hop, 3 * hop]
        terms = [x] + [swap(x, axes, h) for h in hops]
        hop *= 1 + len(hops)
    return terms


def swap(x, axes, hop):
    size = math.prod(lax.axis_size(a) for a in axes)
    return lax.ppermute(x, axes, [(i, i ^ hop) for i in range(size)])


def after(x, y):
    return lax.optimization_barrier((x, y))


def fast(psi_one, psi_two, left, right, table, batch, scale):
    op, core = ("op",), ("help",)
    psi = (psi_one, psi_two)
    waves = []
    far = [swap(x, op, 2) for x in psi]
    later, left = after(psi, left)
    near = [[psi[v], swap(later[v], op, 1), far[v], swap(far[v], op, 1)] for v in range(2)]
    for v in range(2):
        waves += near[v] + [swap(x, core, 1) for x in near[v]]
    *parts, dots = fast_products(batch, table, left, right, waves)
    first = [swap(x, op, k + 1) for k, x in enumerate(parts[1:4])]
    second = [swap(x, op, k + 1) for k, x in enumerate(parts[5:8])]
    terms = terms_of(all_dots(dots, first), ("sec", "help"))
    sigma_one = finish(psi_one.shape, parts[0], first)
    second, sigma_one = after(second, sigma_one)
    sigma_two = finish(psi_two.shape, parts[4], second)
    return sigma_one, sigma_two, subspace_of(scale, terms)


def general(psi_one, psi_two, left, right, table, batch, scale):
    n_op = lax.axis_size("op")
    me = lax.axis_index("op")
    own = jnp.stack([psi_one, psi_two])
    waves = lax.all_gather(own, ("op", "help"), axis=2, tiled=True)
    sums = jnp.swapaxes(any_products(batch, table, left, right, waves), 0, 1)
    total = jnp.take(sums, me, axis=2)
    for k in range(1, n_op):
        sent = jnp.take(sums, (me + k) % n_op, axis=2).astype(BF16)
        moved = lax.ppermute(sent, "op", [(i, (i + k) % n_op) for i in range(n_op)])
        total = total + moved.astype(F32)
    rows = psi_one.shape[1]
    parts = waves.reshape(*waves.shape[:2], n_op, 2, rows, waves.shape[-1])
    mine = jnp.take(parts, lax.axis_index("help"), axis=3).astype(F32)
    dots = jnp.einsum("vsoab,wsoab->vw", mine, sums, precision=lax.Precision.HIGHEST)
    return total[0], total[1], lax.psum(dots, ("op", "sec", "help")) * scale


def local(
    psi_one,
    psi_two,
    left_blocks,
    right_blocks,
    task_in,
    task_out,
    task_left,
    task_right,
    task_count,
):
    sectors, rows, width = psi_one.shape
    ops = left_blocks.shape[0]
    slots = task_in.shape[-1]
    n_op = lax.axis_size("op")
    me = lax.axis_index("op")
    helper = lax.axis_index("help")
    slot = jnp.arange(slots, dtype=jnp.int32)
    flat = lambda t: t.reshape(slots)
    live = task_count.reshape(())
    block = jnp.where(slot < live, flat(task_in) * ops + flat(task_left), sectors * ops)
    state = jnp.where(slot == 0, me, jnp.where(slot == 1, helper, live)).astype(jnp.int32)
    table = jnp.stack([block, flat(task_right), flat(task_out), state])
    lefts = left_blocks.reshape(ops, n_op, 2, rows, width)
    left = jnp.take(lefts, helper, axis=2)
    right = jnp.swapaxes(right_blocks, 1, 2)
    batch = math.gcd(slots, 16)
    scale = 1.0 / math.sqrt(sectors * lax.axis_size("sec") * width * width)
    way = fast if n_op == 4 and rows % 16 == 0 else general
    return way(psi_one, psi_two, left, right, table, batch, scale)


def solution(mesh):
    placed = (
        P(("groups", "sec"), ("op", "help"), None),
        P(("groups", "sec"), ("op", "help"), None),
        P(("groups", "op"), None, None),
        P(("groups", "op"), None, None),
        P(("groups", "op"), "sec", None),
        P(("groups", "op"), "sec", None),
        P(("groups", "op"), "sec", None),
        P(("groups", "op"), "sec", None),
        P(("groups", "op"), "sec"),
    )
    return jax.shard_map(
        local,
        mesh=mesh,
        in_specs=placed,
        out_specs=(
            P(("groups", "sec"), ("op", "help"), None),
            P(("groups", "sec"), ("op", "help"), None),
            P("groups", None),
        ),
        check_vma=False,
    )
```

```python
import functools
import math

import jax
import jax.numpy as jnp
from jax import lax
from jax.experimental import pallas as pl
from jax.experimental.pallas import tpu as pltpu
from jax.sharding import PartitionSpec as P

F32 = jnp.float32
BF16 = jnp.bfloat16
SCALARS = pl.BlockSpec(memory_space=pltpu.SMEM)
VECTORS = pl.BlockSpec(memory_space=pltpu.VMEM)
MIB = 1024 * 1024


def call(kernel, outs, args, n_scalars, mib, name, scratch=(), flops=0):
    return pl.pallas_call(
        kernel,
        out_shape=outs,
        in_specs=[SCALARS] * n_scalars + [VECTORS] * (len(args) - n_scalars),
        out_specs=jax.tree.map(lambda _: VECTORS, outs),
        scratch_shapes=list(scratch),
        compiler_params=pltpu.CompilerParams(vmem_limit_bytes=mib * MIB),
        cost_estimate=pl.CostEstimate(flops=flops, bytes_accessed=0, transcendentals=0) if flops else None,
        name=name,
    )(*args)


def tile_of(x):
    total = None
    for r in range(0, x.shape[0], 8):
        for c in range(0, x.shape[1], 128):
            part = x[r : r + 8, c : c + 128]
            total = part if total is None else total + part
    return total


def dots_of(me, near, sums):
    sectors, n_op = sums.shape[0], sums.shape[2]
    dots = [[None, None], [None, None]]
    for k in range(n_op):
        for c in range(sectors):
            parts = [sums[c, w, me ^ k] for w in range(2)]
            for v in range(2):
                wave = near[v][k][c].astype(F32)
                for w in range(2):
                    part = tile_of(wave * parts[w])
                    dots[v][w] = part if dots[v][w] is None else dots[v][w] + part
    rows = [jnp.sum(dots[v][w], axis=0, keepdims=True) for v in range(2) for w in range(2)]
    return jnp.concatenate(rows + [jnp.zeros((4, 128), F32)])


def to_wire(tile, width):
    high = tile.astype(BF16).astype(F32)
    middle = (tile - high).astype(BF16).astype(F32)
    low = tile - high - middle
    parts = jnp.concatenate([high[:4], middle[:4], low[:4], jnp.zeros((4, 128), F32)])
    return jnp.concatenate([parts] * (width // 128), axis=1).astype(BF16)


def from_wire(ref, at):
    parts = ref[at:, :128].astype(F32)
    four = parts[0:4] + parts[4:8] + parts[8:12]
    return jnp.concatenate([four, jnp.zeros((4, 128), F32)])


def add_tasks(batch, table, left_ref, right_ref, waves, inner, sums):
    sectors, _, n_op, rows, width = sums.shape
    ops, half = right_ref.shape[0], n_op * rows
    left = left_ref[...].reshape(ops * half, width)
    for a in range(sectors):
        for v in range(2):
            found = jnp.dot(left, waves[v, a], preferred_element_type=F32).astype(BF16)
            inner[pl.ds(a * ops, ops), v] = found.reshape(ops, half, width)
    inner[sectors * ops] = jnp.zeros((2, half, width), BF16)
    sums[...] = jnp.zeros_like(sums)

    def step(g, carry):
        for i in range(batch):
            t = g * batch + i
            block = inner[table[0, t]].reshape(2 * half, width)
            found = jnp.dot(block, right_ref[table[1, t]], preferred_element_type=F32)
            sums[table[2, t]] += found.reshape(2, n_op, rows, width)
        return carry

    lax.fori_loop(0, (table[3, 2] + batch - 1) // batch, step, 0)


def fast_kernel(batch, table, left_ref, right_ref, *refs):
    waves_in, refs = refs[:16], refs[16:]
    *outs, dots_ref, waves, inner, sums = refs
    rows = sums.shape[3]
    me, helper = table[3, 0], table[3, 1]
    for v in range(2):
        for k in range(4):
            for other in range(2):
                owner = helper if other == 0 else 1 - helper
                at = pl.multiple_of(((me ^ k) * 2 + owner) * rows, rows)
                waves[v, :, pl.ds(at, rows), :] = waves_in[v * 8 + other * 4 + k][...]
    add_tasks(batch, table, left_ref, right_ref, waves, inner, sums)
    n = sums.shape[0] * rows
    for k in range(4):
        part = sums[:, 0, me ^ k].reshape(n, -1)
        outs[k][:n] = part if k == 0 else part.astype(BF16)
    for i, k in enumerate((0, 2)):
        outs[4 + i][...] = sums[:, 1, me ^ k].reshape(n, -1)
    for i, k in enumerate((1, 3)):
        outs[6][i * n : (i + 1) * n] = sums[:, 1, me ^ k].reshape(n, -1).astype(BF16)
    tile = dots_of(me, (waves_in[:4], waves_in[8:12]), sums)
    dots_ref[...] = tile
    wire = to_wire(tile, sums.shape[-1])
    for k in range(1, 4):
        outs[k][n:] = wire


def fast_products(batch, table, left, right, waves):
    ops, n_op, rows, width = left.shape
    sectors = waves[0].shape[0]
    n = sectors * rows
    own = jax.ShapeDtypeStruct((n, width), F32)
    outs = [own] + [jax.ShapeDtypeStruct((n + 16, width), BF16)] * 3
    outs += [own, own, jax.ShapeDtypeStruct((2 * n, width), BF16)]
    outs.append(jax.ShapeDtypeStruct((8, 128), F32))
    scratch = [
        pltpu.VMEM((2, sectors, width, width), BF16),
        pltpu.VMEM((sectors * ops + 1, 2, n_op * rows, width), BF16),
        pltpu.VMEM((sectors, 2, n_op, rows, width), F32),
    ]
    kernel = functools.partial(fast_kernel, batch)
    return call(kernel, outs, [table, left, right, *waves], 1, 20, "products", scratch)


def any_kernel(batch, table, left_ref, right_ref, waves, sums, inner):
    add_tasks(batch, table, left_ref, right_ref, waves, inner, sums)


def any_products(batch, table, left, right, waves):
    ops, n_op, rows, width = left.shape
    sectors = waves.shape[1]
    out = jax.ShapeDtypeStruct((sectors, 2, n_op, rows, width), F32)
    scratch = [pltpu.VMEM((sectors * ops + 1, 2, n_op * rows, width), BF16)]
    kernel = functools.partial(any_kernel, batch)
    return call(kernel, out, [table, left, right, waves], 1, 20, "products", scratch)


def add_up(terms):
    while len(terms) > 1:
        terms = [a + b for a, b in zip(terms[::2], terms[1::2])]
    return terms[0]


def pair_kernel(cross, received, out):
    n = cross.shape[0]
    out[...] = (cross[...] + received[n:].astype(F32)).astype(BF16)


def pair_sums(cross, received):
    out = jax.ShapeDtypeStruct(cross.shape, BF16)
    return call(pair_kernel, out, [cross, received], 0, 2, "pair_sums")


def dots_kernel(n, own, *refs):
    refs[-1][...] = add_up([own[...]] + [from_wire(r, n) for r in refs[:-1]])


def all_dots(own, received):
    kernel = functools.partial(dots_kernel, received[0].shape[0] - 16)
    return call(kernel, jax.ShapeDtypeStruct((8, 128), F32), [own, *received], 0, 1, "all_dots")


def finish_kernel(scale, n, mine, *refs):
    received, terms = refs[:n], refs[n:]
    out = terms[-1] if scale is None else terms[-2]
    rows = mine.shape[0]
    total = mine[...]
    for part in received:
        total = total + part[:rows].astype(F32)
    out[...] = total.reshape(out.shape)
    if scale is not None:
        write_matrix(terms[-1], add_up([t[...] for t in terms[:-2]]), scale)


def write_matrix(out, tile, scale):
    whole = jnp.sum(tile, axis=1, keepdims=True) * scale
    for v in range(2):
        for w in range(2):
            out[v : v + 1, w : w + 1] = whole[2 * v + w : 2 * v + w + 1]


def finish(shape, mine, received, terms=(), scale=None):
    outs = [jax.ShapeDtypeStruct(shape, F32)]
    if terms:
        outs.append(jax.ShapeDtypeStruct((2, 2), F32))
    kernel = functools.partial(finish_kernel, scale, len(received))
    return call(kernel, outs, [mine, *received, *terms], 0, 4, "finish")


def terms_of(x, axes):
    size = math.prod(lax.axis_size(a) for a in axes)
    terms, hop = [x], 1
    while hop < size:
        x = add_up(terms)
        hops = [hop] if hop * 2 == size else [hop, 2 * hop, 3 * hop]
        terms = [x] + [swap(x, axes, h) for h in hops]
        hop *= 1 + len(hops)
    return terms


def swap(x, axes, hop):
    size = math.prod(lax.axis_size(a) for a in axes)
    return lax.ppermute(x, axes, [(i, i ^ hop) for i in range(size)])


def after(x, y):
    return lax.optimization_barrier((x, y))


def fast(psi_one, psi_two, left, right, table, batch, scale):
    op, core = ("op",), ("help",)
    psi = (psi_one, psi_two)
    waves = []
    far = [swap(x, op, 2) for x in psi]
    near = [[psi[v], swap(psi[v], op, 1), far[v], swap(far[v], op, 1)] for v in range(2)]
    for v in range(2):
        waves += near[v] + [swap(x, core, 1) for x in near[v]]
    *parts, dots = fast_products(batch, table, left, right, waves)
    paired = swap(parts[6], op, 1)
    first = [swap(x, op, k + 1) for k, x in enumerate(parts[1:4])]
    paired, first[2] = after(paired, first[2])
    far_sum = swap(pair_sums(parts[5], paired), op, 2)
    terms = terms_of(all_dots(dots, first), ("sec", "help"))
    (sigma_one,) = finish(psi_one.shape, parts[0], first)
    far_sum, sigma_one = after(far_sum, sigma_one)
    sigma_two, subspace = finish(psi_two.shape, parts[4], [paired, far_sum], terms, scale)
    return sigma_one, sigma_two, subspace


def general(psi_one, psi_two, left, right, table, batch, scale):
    n_op = lax.axis_size("op")
    me = lax.axis_index("op")
    own = jnp.stack([psi_one, psi_two])
    waves = lax.all_gather(own, ("op", "help"), axis=2, tiled=True)
    sums = jnp.swapaxes(any_products(batch, table, left, right, waves), 0, 1)
    total = jnp.take(sums, me, axis=2)
    for k in range(1, n_op):
        sent = jnp.take(sums, (me + k) % n_op, axis=2).astype(BF16)
        moved = lax.ppermute(sent, "op", [(i, (i + k) % n_op) for i in range(n_op)])
        total = total + moved.astype(F32)
    rows = psi_one.shape[1]
    parts = waves.reshape(*waves.shape[:2], n_op, 2, rows, waves.shape[-1])
    mine = jnp.take(parts, lax.axis_index("help"), axis=3).astype(F32)
    dots = jnp.einsum("vsoab,wsoab->vw", mine, sums, precision=lax.Precision.HIGHEST)
    return total[0], total[1], lax.psum(dots, ("op", "sec", "help")) * scale


def local(
    psi_one,
    psi_two,
    left_blocks,
    right_blocks,
    task_in,
    task_out,
    task_left,
    task_right,
    task_count,
):
    sectors, rows, width = psi_one.shape
    ops = left_blocks.shape[0]
    slots = task_in.shape[-1]
    n_op = lax.axis_size("op")
    me = lax.axis_index("op")
    helper = lax.axis_index("help")
    slot = jnp.arange(slots, dtype=jnp.int32)
    flat = lambda t: t.reshape(slots)
    live = task_count.reshape(())
    block = jnp.where(slot < live, flat(task_in) * ops + flat(task_left), sectors * ops)
    state = jnp.where(slot == 0, me, jnp.where(slot == 1, helper, live)).astype(jnp.int32)
    table = jnp.stack([block, flat(task_right), flat(task_out), state])
    lefts = left_blocks.reshape(ops, n_op, 2, rows, width)
    left = jnp.take(lefts, helper, axis=2)
    right = jnp.swapaxes(right_blocks, 1, 2)
    batch = math.gcd(slots, 32)
    scale = 1.0 / math.sqrt(sectors * lax.axis_size("sec") * width * width)
    way = fast if n_op == 4 and rows % 16 == 0 else general
    return way(psi_one, psi_two, left, right, table, batch, scale)


def solution(mesh):
    placed = (
        P(("groups", "sec"), ("op", "help"), None),
        P(("groups", "sec"), ("op", "help"), None),
        P(("groups", "op"), None, None),
        P(("groups", "op"), None, None),
        P(("groups", "op"), "sec", None),
        P(("groups", "op"), "sec", None),
        P(("groups", "op"), "sec", None),
        P(("groups", "op"), "sec", None),
        P(("groups", "op"), "sec"),
    )
    return jax.shard_map(
        local,
        mesh=mesh,
        in_specs=placed,
        out_specs=(
            P(("groups", "sec"), ("op", "help"), None),
            P(("groups", "sec"), ("op", "help"), None),
            P("groups", None),
        ),
        check_vma=False,
    )
```

```python
import functools
import math

import jax
import jax.numpy as jnp
from jax import lax
from jax.experimental import pallas as pl
from jax.experimental.pallas import tpu as pltpu
from jax.sharding import PartitionSpec as P

F32 = jnp.float32
BF16 = jnp.bfloat16
SCALARS = pl.BlockSpec(memory_space=pltpu.SMEM)
VECTORS = pl.BlockSpec(memory_space=pltpu.VMEM)
MIB = 1024 * 1024


def call(kernel, outs, args, n_scalars, mib, name, scratch=(), flops=0):
    return pl.pallas_call(
        kernel,
        out_shape=outs,
        in_specs=[SCALARS] * n_scalars + [VECTORS] * (len(args) - n_scalars),
        out_specs=jax.tree.map(lambda _: VECTORS, outs),
        scratch_shapes=list(scratch),
        compiler_params=pltpu.CompilerParams(vmem_limit_bytes=mib * MIB),
        cost_estimate=pl.CostEstimate(flops=flops, bytes_accessed=0, transcendentals=0) if flops else None,
        name=name,
    )(*args)


def tile_of(x):
    total = None
    for r in range(0, x.shape[0], 8):
        for c in range(0, x.shape[1], 128):
            part = x[r : r + 8, c : c + 128]
            total = part if total is None else total + part
    return total


def dots_of(me, near, sums):
    sectors, n_op = sums.shape[0], sums.shape[2]
    dots = [[None, None], [None, None]]
    for k in range(n_op):
        for c in range(sectors):
            parts = [sums[c, w, me ^ k] for w in range(2)]
            for v in range(2):
                wave = near[v][k][c].astype(F32)
                for w in range(2):
                    part = tile_of(wave * parts[w])
                    dots[v][w] = part if dots[v][w] is None else dots[v][w] + part
    rows = [jnp.sum(dots[v][w], axis=0, keepdims=True) for v in range(2) for w in range(2)]
    return jnp.concatenate(rows + [jnp.zeros((4, 128), F32)])


def to_wire(tile, width):
    high = tile.astype(BF16).astype(F32)
    middle = (tile - high).astype(BF16).astype(F32)
    low = tile - high - middle
    parts = jnp.concatenate([high[:4], middle[:4], low[:4], jnp.zeros((4, 128), F32)])
    return jnp.concatenate([parts] * (width // 128), axis=1).astype(BF16)


def from_wire(ref, at):
    parts = ref[at:, :128].astype(F32)
    four = parts[0:4] + parts[4:8] + parts[8:12]
    return jnp.concatenate([four, jnp.zeros((4, 128), F32)])


def add_tasks(batch, table, left_ref, right_ref, waves, inner, sums, odd):
    sectors, _, n_op, rows, width = sums.shape
    ops, half = right_ref.shape[0], n_op * rows
    left = left_ref[...].reshape(ops * half, width)
    for a in range(sectors):
        for v in range(2):
            found = jnp.dot(left, waves[v, a], preferred_element_type=F32).astype(BF16)
            inner[pl.ds(a * ops, ops), v] = found.reshape(ops, half, width)
    inner[sectors * ops] = jnp.zeros((2, half, width), BF16)
    sums[...] = jnp.zeros_like(sums)
    odd[...] = jnp.zeros_like(odd)

    def step(g, carry):
        for i in range(batch):
            t = g * batch + i
            block = inner[table[0, t]].reshape(2 * half, width)
            found = jnp.dot(block, right_ref[table[1, t]], preferred_element_type=F32)
            total = odd if i % 2 else sums
            total[table[2, t]] += found.reshape(2, n_op, rows, width)
        return carry

    lax.fori_loop(0, (table[3, 2] + batch - 1) // batch, step, 0)
    sums[...] += odd[...]


def fast_kernel(batch, table, left_ref, right_ref, *refs):
    waves_in, refs = refs[:16], refs[16:]
    *outs, dots_ref, waves, inner, sums, odd = refs
    rows = sums.shape[3]
    me, helper = table[3, 0], table[3, 1]
    for v in range(2):
        for k in range(4):
            for other in range(2):
                owner = helper if other == 0 else 1 - helper
                at = pl.multiple_of(((me ^ k) * 2 + owner) * rows, rows)
                waves[v, :, pl.ds(at, rows), :] = waves_in[v * 8 + other * 4 + k][...]
    add_tasks(batch, table, left_ref, right_ref, waves, inner, sums, odd)
    n = sums.shape[0] * rows
    for k in range(4):
        part = sums[:, 0, me ^ k].reshape(n, -1)
        outs[k][:n] = part if k == 0 else part.astype(BF16)
    for i, k in enumerate((0, 2)):
        outs[4 + i][...] = sums[:, 1, me ^ k].reshape(n, -1)
    for i, k in enumerate((1, 3)):
        outs[6][i * n : (i + 1) * n] = sums[:, 1, me ^ k].reshape(n, -1).astype(BF16)
    tile = dots_of(me, (waves_in[:4], waves_in[8:12]), sums)
    dots_ref[...] = tile
    wire = to_wire(tile, sums.shape[-1])
    for k in range(1, 4):
        outs[k][n:] = wire


def fast_products(batch, table, left, right, waves):
    ops, n_op, rows, width = left.shape
    sectors = waves[0].shape[0]
    n = sectors * rows
    own = jax.ShapeDtypeStruct((n, width), F32)
    outs = [own] + [jax.ShapeDtypeStruct((n + 16, width), BF16)] * 3
    outs += [own, own, jax.ShapeDtypeStruct((2 * n, width), BF16)]
    outs.append(jax.ShapeDtypeStruct((8, 128), F32))
    scratch = [
        pltpu.VMEM((2, sectors, width, width), BF16),
        pltpu.VMEM((sectors * ops + 1, 2, n_op * rows, width), BF16),
        pltpu.VMEM((sectors, 2, n_op, rows, width), F32),
        pltpu.VMEM((sectors, 2, n_op, rows, width), F32),
    ]
    kernel = functools.partial(fast_kernel, batch)
    return call(kernel, outs, [table, left, right, *waves], 1, 20, "products", scratch)


def any_kernel(batch, table, left_ref, right_ref, waves, sums, inner, odd):
    add_tasks(batch, table, left_ref, right_ref, waves, inner, sums, odd)


def any_products(batch, table, left, right, waves):
    ops, n_op, rows, width = left.shape
    sectors = waves.shape[1]
    out = jax.ShapeDtypeStruct((sectors, 2, n_op, rows, width), F32)
    scratch = [pltpu.VMEM((sectors * ops + 1, 2, n_op * rows, width), BF16), pltpu.VMEM(out.shape, F32)]
    kernel = functools.partial(any_kernel, batch)
    return call(kernel, out, [table, left, right, waves], 1, 20, "products", scratch)


def add_up(terms):
    while len(terms) > 1:
        terms = [a + b for a, b in zip(terms[::2], terms[1::2])]
    return terms[0]


def pair_kernel(cross, received, out):
    n = cross.shape[0]
    out[...] = (cross[...] + received[n:].astype(F32)).astype(BF16)


def pair_sums(cross, received):
    out = jax.ShapeDtypeStruct(cross.shape, BF16)
    return call(pair_kernel, out, [cross, received], 0, 2, "pair_sums")


def dots_kernel(n, own, *refs):
    refs[-1][...] = add_up([own[...]] + [from_wire(r, n) for r in refs[:-1]])


def all_dots(own, received):
    kernel = functools.partial(dots_kernel, received[0].shape[0] - 16)
    return call(kernel, jax.ShapeDtypeStruct((8, 128), F32), [own, *received], 0, 1, "all_dots")


def finish_kernel(scale, n, mine, *refs):
    received, terms = refs[:n], refs[n:]
    out = terms[-1] if scale is None else terms[-2]
    rows = mine.shape[0]
    total = mine[...]
    for part in received:
        total = total + part[:rows].astype(F32)
    out[...] = total.reshape(out.shape)
    if scale is not None:
        write_matrix(terms[-1], add_up([t[...] for t in terms[:-2]]), scale)


def write_matrix(out, tile, scale):
    whole = jnp.sum(tile, axis=1, keepdims=True) * scale
    for v in range(2):
        for w in range(2):
            out[v : v + 1, w : w + 1] = whole[2 * v + w : 2 * v + w + 1]


def finish(shape, mine, received, terms=(), scale=None):
    outs = [jax.ShapeDtypeStruct(shape, F32)]
    if terms:
        outs.append(jax.ShapeDtypeStruct((2, 2), F32))
    kernel = functools.partial(finish_kernel, scale, len(received))
    return call(kernel, outs, [mine, *received, *terms], 0, 4, "finish")


def terms_of(x, axes):
    size = math.prod(lax.axis_size(a) for a in axes)
    terms, hop = [x], 1
    while hop < size:
        x = add_up(terms)
        hops = [hop] if hop * 2 == size else [hop, 2 * hop, 3 * hop]
        terms = [x] + [swap(x, axes, h) for h in hops]
        hop *= 1 + len(hops)
    return terms


def swap(x, axes, hop):
    size = math.prod(lax.axis_size(a) for a in axes)
    return lax.ppermute(x, axes, [(i, i ^ hop) for i in range(size)])


def after(x, y):
    return lax.optimization_barrier((x, y))


def fast(psi_one, psi_two, left, right, table, batch, scale):
    op, core = ("op",), ("help",)
    psi = (psi_one, psi_two)
    waves = []
    far = [swap(x, op, 2) for x in psi]
    near = [[psi[v], swap(psi[v], op, 1), far[v], swap(far[v], op, 1)] for v in range(2)]
    late, near[0][3] = after(psi, near[0][3])
    for v in range(2):
        near[v][0] = late[v]
    for v in range(2):
        waves += near[v] + [swap(x, core, 1) for x in near[v]]
    *parts, dots = fast_products(batch, table, left, right, waves)
    paired = swap(parts[6], op, 1)
    first = [swap(x, op, k + 1) for k, x in enumerate(parts[1:4])]
    paired, first[2] = after(paired, first[2])
    far_sum = swap(pair_sums(parts[5], paired), op, 2)
    terms = terms_of(all_dots(dots, first), ("sec", "help"))
    (sigma_one,) = finish(psi_one.shape, parts[0], first)
    far_sum, sigma_one = after(far_sum, sigma_one)
    sigma_two, subspace = finish(psi_two.shape, parts[4], [paired, far_sum], terms, scale)
    return sigma_one, sigma_two, subspace


def general(psi_one, psi_two, left, right, table, batch, scale):
    n_op = lax.axis_size("op")
    me = lax.axis_index("op")
    own = jnp.stack([psi_one, psi_two])
    waves = lax.all_gather(own, ("op", "help"), axis=2, tiled=True)
    sums = jnp.swapaxes(any_products(batch, table, left, right, waves), 0, 1)
    total = jnp.take(sums, me, axis=2)
    for k in range(1, n_op):
        sent = jnp.take(sums, (me + k) % n_op, axis=2).astype(BF16)
        moved = lax.ppermute(sent, "op", [(i, (i + k) % n_op) for i in range(n_op)])
        total = total + moved.astype(F32)
    rows = psi_one.shape[1]
    parts = waves.reshape(*waves.shape[:2], n_op, 2, rows, waves.shape[-1])
    mine = jnp.take(parts, lax.axis_index("help"), axis=3).astype(F32)
    dots = jnp.einsum("vsoab,wsoab->vw", mine, sums, precision=lax.Precision.HIGHEST)
    return total[0], total[1], lax.psum(dots, ("op", "sec", "help")) * scale


def local(
    psi_one,
    psi_two,
    left_blocks,
    right_blocks,
    task_in,
    task_out,
    task_left,
    task_right,
    task_count,
):
    sectors, rows, width = psi_one.shape
    ops = left_blocks.shape[0]
    slots = task_in.shape[-1]
    n_op = lax.axis_size("op")
    me = lax.axis_index("op")
    helper = lax.axis_index("help")
    slot = jnp.arange(slots, dtype=jnp.int32)
    flat = lambda t: t.reshape(slots)
    live = task_count.reshape(())
    block = jnp.where(slot < live, flat(task_in) * ops + flat(task_left), sectors * ops)
    state = jnp.where(slot == 0, me, jnp.where(slot == 1, helper, live)).astype(jnp.int32)
    table = jnp.stack([block, flat(task_right), flat(task_out), state])
    lefts = left_blocks.reshape(ops, n_op, 2, rows, width)
    left = jnp.take(lefts, helper, axis=2)
    right = jnp.swapaxes(right_blocks, 1, 2)
    batch = math.gcd(slots, 32)
    scale = 1.0 / math.sqrt(sectors * lax.axis_size("sec") * width * width)
    way = fast if n_op == 4 and rows % 16 == 0 else general
    return way(psi_one, psi_two, left, right, table, batch, scale)


def solution(mesh):
    placed = (
        P(("groups", "sec"), ("op", "help"), None),
        P(("groups", "sec"), ("op", "help"), None),
        P(("groups", "op"), None, None),
        P(("groups", "op"), None, None),
        P(("groups", "op"), "sec", None),
        P(("groups", "op"), "sec", None),
        P(("groups", "op"), "sec", None),
        P(("groups", "op"), "sec", None),
        P(("groups", "op"), "sec"),
    )
    return jax.shard_map(
        local,
        mesh=mesh,
        in_specs=placed,
        out_specs=(
            P(("groups", "sec"), ("op", "help"), None),
            P(("groups", "sec"), ("op", "help"), None),
            P("groups", None),
        ),
        check_vma=False,
    )
```

```python
import functools
import math

import jax
import jax.numpy as jnp
from jax import lax
from jax.experimental import pallas as pl
from jax.experimental.pallas import tpu as pltpu
from jax.sharding import PartitionSpec as P

F32 = jnp.float32
BF16 = jnp.bfloat16
SCALARS = pl.BlockSpec(memory_space=pltpu.SMEM)
VECTORS = pl.BlockSpec(memory_space=pltpu.VMEM)
MIB = 1024 * 1024


def call(kernel, outs, args, n_scalars, mib, name, scratch=(), flops=0):
    return pl.pallas_call(
        kernel,
        out_shape=outs,
        in_specs=[SCALARS] * n_scalars + [VECTORS] * (len(args) - n_scalars),
        out_specs=jax.tree.map(lambda _: VECTORS, outs),
        scratch_shapes=list(scratch),
        compiler_params=pltpu.CompilerParams(vmem_limit_bytes=mib * MIB),
        cost_estimate=pl.CostEstimate(flops=flops, bytes_accessed=0, transcendentals=0) if flops else None,
        name=name,
    )(*args)


def tile_of(x):
    total = None
    for r in range(0, x.shape[0], 8):
        for c in range(0, x.shape[1], 128):
            part = x[r : r + 8, c : c + 128]
            total = part if total is None else total + part
    return total


def dots_of(me, near, sums):
    sectors, n_op = sums.shape[0], sums.shape[2]
    dots = [[None, None], [None, None]]
    for k in range(n_op):
        for c in range(sectors):
            parts = [sums[c, w, me ^ k] for w in range(2)]
            for v in range(2):
                wave = near[v][k][c].astype(F32)
                for w in range(2):
                    part = tile_of(wave * parts[w])
                    dots[v][w] = part if dots[v][w] is None else dots[v][w] + part
    rows = [jnp.sum(dots[v][w], axis=0, keepdims=True) for v in range(2) for w in range(2)]
    return jnp.concatenate(rows + [jnp.zeros((4, 128), F32)])


def to_wire(tile, width):
    high = tile.astype(BF16).astype(F32)
    middle = (tile - high).astype(BF16).astype(F32)
    low = tile - high - middle
    parts = jnp.concatenate([high[:4], middle[:4], low[:4], jnp.zeros((4, 128), F32)])
    return jnp.concatenate([parts] * (width // 128), axis=1).astype(BF16)


def from_wire(ref, at):
    parts = ref[at:, :128].astype(F32)
    four = parts[0:4] + parts[4:8] + parts[8:12]
    return jnp.concatenate([four, jnp.zeros((4, 128), F32)])


def add_tasks(batch, table, left_ref, right_ref, waves, inner, sums, odd):
    sectors, _, n_op, rows, width = sums.shape
    ops, half = right_ref.shape[0], n_op * rows
    left = left_ref[...].reshape(ops * half, width)
    for a in range(sectors):
        for v in range(2):
            found = jnp.dot(left, waves[v, a], preferred_element_type=F32).astype(BF16)
            inner[pl.ds(a * ops, ops), v] = found.reshape(ops, half, width)
    inner[sectors * ops] = jnp.zeros((2, half, width), BF16)
    sums[...] = jnp.zeros_like(sums)
    odd[...] = jnp.zeros_like(odd)

    def step(g, carry):
        for i in range(batch):
            t = g * batch + i
            block = inner[table[0, t]].reshape(2 * half, width)
            found = jnp.dot(block, right_ref[table[1, t]], preferred_element_type=F32)
            total = odd if i % 2 else sums
            total[table[2, t]] += found.reshape(2, n_op, rows, width)
        return carry

    lax.fori_loop(0, (table[3, 2] + batch - 1) // batch, step, 0)
    sums[...] += odd[...]


def fast_kernel(batch, table, left_ref, right_ref, *refs):
    waves_in, refs = refs[:16], refs[16:]
    *outs, dots_ref, waves, inner, sums, odd = refs
    rows = sums.shape[3]
    me, helper = table[3, 0], table[3, 1]
    for v in range(2):
        for k in range(4):
            for other in range(2):
                owner = helper if other == 0 else 1 - helper
                at = pl.multiple_of(((me ^ k) * 2 + owner) * rows, rows)
                waves[v, :, pl.ds(at, rows), :] = waves_in[v * 8 + other * 4 + k][...]
    add_tasks(batch, table, left_ref, right_ref, waves, inner, sums, odd)
    n = sums.shape[0] * rows
    for k in range(4):
        part = sums[:, 0, me ^ k].reshape(n, -1)
        outs[k][:n] = part if k == 0 else part.astype(BF16)
    for i, k in enumerate((0, 2)):
        outs[4 + i][...] = sums[:, 1, me ^ k].reshape(n, -1)
    for i, k in enumerate((1, 3)):
        outs[6][i * n : (i + 1) * n] = sums[:, 1, me ^ k].reshape(n, -1).astype(BF16)
    tile = dots_of(me, (waves_in[:4], waves_in[8:12]), sums)
    dots_ref[...] = tile
    wire = to_wire(tile, sums.shape[-1])
    for k in range(1, 4):
        outs[k][n:] = wire


def fast_products(batch, table, left, right, waves):
    ops, n_op, rows, width = left.shape
    sectors = waves[0].shape[0]
    n = sectors * rows
    own = jax.ShapeDtypeStruct((n, width), F32)
    outs = [own] + [jax.ShapeDtypeStruct((n + 16, width), BF16)] * 3
    outs += [own, own, jax.ShapeDtypeStruct((2 * n, width), BF16)]
    outs.append(jax.ShapeDtypeStruct((8, 128), F32))
    scratch = [
        pltpu.VMEM((2, sectors, width, width), BF16),
        pltpu.VMEM((sectors * ops + 1, 2, n_op * rows, width), BF16),
        pltpu.VMEM((sectors, 2, n_op, rows, width), F32),
        pltpu.VMEM((sectors, 2, n_op, rows, width), F32),
    ]
    kernel = functools.partial(fast_kernel, batch)
    return call(kernel, outs, [table, left, right, *waves], 1, 20, "products", scratch)


def any_kernel(batch, table, left_ref, right_ref, waves, sums, inner, odd):
    add_tasks(batch, table, left_ref, right_ref, waves, inner, sums, odd)


def any_products(batch, table, left, right, waves):
    ops, n_op, rows, width = left.shape
    sectors = waves.shape[1]
    out = jax.ShapeDtypeStruct((sectors, 2, n_op, rows, width), F32)
    scratch = [pltpu.VMEM((sectors * ops + 1, 2, n_op * rows, width), BF16), pltpu.VMEM(out.shape, F32)]
    kernel = functools.partial(any_kernel, batch)
    return call(kernel, out, [table, left, right, waves], 1, 20, "products", scratch)


def add_up(terms):
    while len(terms) > 1:
        terms = [a + b for a, b in zip(terms[::2], terms[1::2])]
    return terms[0]


def pair_kernel(cross, received, out):
    n = cross.shape[0]
    out[...] = (cross[...] + received[n:].astype(F32)).astype(BF16)


def pair_sums(cross, received):
    out = jax.ShapeDtypeStruct(cross.shape, BF16)
    return call(pair_kernel, out, [cross, received], 0, 2, "pair_sums")


def dots_kernel(n, own, *refs):
    refs[-1][...] = add_up([own[...]] + [from_wire(r, n) for r in refs[:-1]])


def all_dots(own, received):
    kernel = functools.partial(dots_kernel, received[0].shape[0] - 16)
    return call(kernel, jax.ShapeDtypeStruct((8, 128), F32), [own, *received], 0, 1, "all_dots")


def finish_kernel(scale, n, mine, *refs):
    received, terms = refs[:n], refs[n:]
    out = terms[-1] if scale is None else terms[-2]
    rows = mine.shape[0]
    total = mine[...]
    for part in received:
        total = total + part[:rows].astype(F32)
    out[...] = total.reshape(out.shape)
    if scale is not None:
        write_matrix(terms[-1], add_up([t[...] for t in terms[:-2]]), scale)


def write_matrix(out, tile, scale):
    whole = jnp.sum(tile, axis=1, keepdims=True) * scale
    for v in range(2):
        for w in range(2):
            out[v : v + 1, w : w + 1] = whole[2 * v + w : 2 * v + w + 1]


def finish(shape, mine, received, terms=(), scale=None):
    outs = [jax.ShapeDtypeStruct(shape, F32)]
    if terms:
        outs.append(jax.ShapeDtypeStruct((2, 2), F32))
    kernel = functools.partial(finish_kernel, scale, len(received))
    return call(kernel, outs, [mine, *received, *terms], 0, 4, "finish")


def terms_of(x, axes):
    size = math.prod(lax.axis_size(a) for a in axes)
    terms, hop = [x], 1
    while hop < size:
        x = add_up(terms)
        hops = [hop] if hop * 2 == size else [hop, 2 * hop, 3 * hop]
        terms = [x] + [swap(x, axes, h) for h in hops]
        hop *= 1 + len(hops)
    return terms


def swap(x, axes, hop):
    size = math.prod(lax.axis_size(a) for a in axes)
    return lax.ppermute(x, axes, [(i, i ^ hop) for i in range(size)])


def after(x, y):
    return lax.optimization_barrier((x, y))


def fast(psi_one, psi_two, left, right, table, batch, scale):
    op, core = ("op",), ("help",)
    psi = (psi_one, psi_two)
    waves = []
    far = [swap(x, op, 2) for x in psi]
    near = [[psi[v], swap(psi[v], op, 1), far[v], swap(far[v], op, 1)] for v in range(2)]
    late, near[0][3] = after(psi, near[0][3])
    for v in range(2):
        near[v][0] = late[v]
    for v in range(2):
        waves += near[v] + [swap(x, core, 1) for x in near[v]]
    *parts, dots = fast_products(batch, table, left, right, waves)
    paired = swap(parts[6], op, 1)
    first = [swap(x, op, k + 1) for k, x in enumerate(parts[1:4])]
    paired, first[2] = after(paired, first[2])
    far_sum = swap(pair_sums(parts[5], paired), op, 2)
    terms = terms_of(all_dots(dots, first), ("sec", "help"))
    (sigma_one,) = finish(psi_one.shape, parts[0], first)
    sigma_two, subspace = finish(psi_two.shape, parts[4], [paired, far_sum], terms, scale)
    return sigma_one, sigma_two, subspace


def general(psi_one, psi_two, left, right, table, batch, scale):
    n_op = lax.axis_size("op")
    me = lax.axis_index("op")
    own = jnp.stack([psi_one, psi_two])
    waves = lax.all_gather(own, ("op", "help"), axis=2, tiled=True)
    sums = jnp.swapaxes(any_products(batch, table, left, right, waves), 0, 1)
    total = jnp.take(sums, me, axis=2)
    for k in range(1, n_op):
        sent = jnp.take(sums, (me + k) % n_op, axis=2).astype(BF16)
        moved = lax.ppermute(sent, "op", [(i, (i + k) % n_op) for i in range(n_op)])
        total = total + moved.astype(F32)
    rows = psi_one.shape[1]
    parts = waves.reshape(*waves.shape[:2], n_op, 2, rows, waves.shape[-1])
    mine = jnp.take(parts, lax.axis_index("help"), axis=3).astype(F32)
    dots = jnp.einsum("vsoab,wsoab->vw", mine, sums, precision=lax.Precision.HIGHEST)
    return total[0], total[1], lax.psum(dots, ("op", "sec", "help")) * scale


def local(
    psi_one,
    psi_two,
    left_blocks,
    right_blocks,
    task_in,
    task_out,
    task_left,
    task_right,
    task_count,
):
    sectors, rows, width = psi_one.shape
    ops = left_blocks.shape[0]
    slots = task_in.shape[-1]
    n_op = lax.axis_size("op")
    me = lax.axis_index("op")
    helper = lax.axis_index("help")
    slot = jnp.arange(slots, dtype=jnp.int32)
    flat = lambda t: t.reshape(slots)
    live = task_count.reshape(())
    block = jnp.where(slot < live, flat(task_in) * ops + flat(task_left), sectors * ops)
    state = jnp.where(slot == 0, me, jnp.where(slot == 1, helper, live)).astype(jnp.int32)
    table = jnp.stack([block, flat(task_right), flat(task_out), state])
    lefts = left_blocks.reshape(ops, n_op, 2, rows, width)
    left = jnp.take(lefts, helper, axis=2)
    right = jnp.swapaxes(right_blocks, 1, 2)
    batch = math.gcd(slots, 32)
    scale = 1.0 / math.sqrt(sectors * lax.axis_size("sec") * width * width)
    way = fast if n_op == 4 and rows % 16 == 0 else general
    return way(psi_one, psi_two, left, right, table, batch, scale)


def solution(mesh):
    placed = (
        P(("groups", "sec"), ("op", "help"), None),
        P(("groups", "sec"), ("op", "help"), None),
        P(("groups", "op"), None, None),
        P(("groups", "op"), None, None),
        P(("groups", "op"), "sec", None),
        P(("groups", "op"), "sec", None),
        P(("groups", "op"), "sec", None),
        P(("groups", "op"), "sec", None),
        P(("groups", "op"), "sec"),
    )
    return jax.shard_map(
        local,
        mesh=mesh,
        in_specs=placed,
        out_specs=(
            P(("groups", "sec"), ("op", "help"), None),
            P(("groups", "sec"), ("op", "help"), None),
            P("groups", None),
        ),
        check_vma=False,
    )
```
